768 devices in a mesh: dp: 24 (over z, y_hi), outer: 32 (over y_lo, x, core).
Axes of the slice: x: 4, y: 8 (y_hi: 2, y_lo: 4; y = y_hi * 4 + y_lo), z: 12, core: 2. Of those that a mesh axis runs over, the one named last changes fastest.
Arguments:
- images: bfloat16 [344064, 1152], P(('dp', 'outer')), may hold values from -1.1953125 to 1.1953125
- texts: bfloat16 [344064, 1152], P(('dp', 'outer')), may hold values from -1.1953125 to 1.1953125
- positive_index: int32 [768, 448], P(('dp', 'outer')), may hold values from 0 to 447, each once within a row
- log_scale: float32 [1], replicated, may hold values from 0 to 1
- bias: float32 [1], replicated, may hold values from -5 to -1
Outputs:
- row_loss: float32 [344064], P(('dp', 'outer'))
- image_grad: bfloat16 [344064, 1152], P(('dp', 'outer'))
- text_grad: bfloat16 [344064, 1152], P(('dp', 'outer'))
The draws below stay inside these ranges and needn't reach their ends.
Inputs may be any that keep to these rules, and one draw needn't show every extreme that they name: Each row of positive_index is a permutation: every text of a block is the positive of exactly one image of that block.
All inputs are finite; a program needn't handle non-finite values.
Results may differ from the reference program's by a relative error of at most 0.008.
Values may be sent and summed in bfloat16 or wider, within the bound.
No kernel may reach another device: no remote copies, remote signals or barrier semaphores. Data moves between devices by JAX's collectives and lax.ppermute only.
A program may use at most 32 MiB of HBM per device.

```python
import jax
import jax.numpy as jnp
from jax import lax

D = 1152
B = 448
BLOCKS = 768
ROWS = 344064
N_DP = 24
N_OUTER = 32


def shard_levels(own_key, extent, pieces, smallest, top_value):
    def one(position, parts):
        heights = jax.random.uniform(jax.random.fold_in(jax.random.fold_in(own_key, 6), position), (parts,), jnp.float32, smallest / len(pieces), top_value / len(pieces))
        return jnp.repeat(jnp.exp(heights), extent[position] // parts).reshape((-1,) + (1,) * (len(extent) - position - 1))

    gain = one(*pieces[0])
    for cut in pieces[1:]:
        gain = gain * one(*cut)
    return gain


def noise(key, extent, scale, bound, split=(), kind=jnp.bfloat16):
    gain = shard_levels(key, extent, split, -0.22, 0.18) if split else 1.0
    drawn = jax.random.normal(key, extent, jnp.float32) * scale * gain
    return jnp.minimum(jnp.maximum(drawn, -bound), bound).astype(kind)


def setup_inputs(seed: int = 0) -> dict:
    splits = jax.random.split(jax.random.key(seed), 6)
    return {
        "images": noise(splits[0], (ROWS, D), 0.17, 1.1953125, ((0, 768),)),
        "texts": noise(splits[1], (ROWS, D), 0.17, 1.1953125, ((0, 768),)),
        "positive_index": jax.vmap(lambda own: jax.random.permutation(own, B))(jax.random.split(splits[2], BLOCKS)).reshape((BLOCKS, B)).astype(jnp.int32),
        "log_scale": jnp.clip(jax.random.uniform(splits[3], (1,), jnp.float32, 0.0, 1.0), 0.0, 1.0),
        "bias": jnp.clip(jax.random.uniform(splits[4], (1,), jnp.float32, -5.0, -1.0), -5.0, -1.0),
    }


def block_terms(args_block):
    image_rows, own_text, cycle_text, pod_text, positive_row, temper, offset_b = args_block
    row_count = image_rows.shape[0]
    positive_mask = positive_row[:, None] == lax.broadcasted_iota(jnp.int32, (row_count, row_count), 1)
    own_logits = temper * jnp.dot(image_rows, own_text.T, preferred_element_type=jnp.float32) + offset_b
    cycle_logits = temper * jnp.dot(image_rows, cycle_text.T, preferred_element_type=jnp.float32) + offset_b
    pod_logits = temper * jnp.dot(image_rows, pod_text.T, preferred_element_type=jnp.float32) + offset_b
    signed = jnp.where(positive_mask, own_logits, -own_logits)
    loss_sum = jnp.sum(jax.nn.softplus(-signed), axis=1)
    loss_sum = loss_sum + jnp.sum(jax.nn.softplus(cycle_logits), axis=1) + jnp.sum(jax.nn.softplus(pod_logits), axis=1)
    row_loss = loss_sum / (3.0 * row_count)
    own_coeff = (temper * (jax.nn.sigmoid(own_logits) - positive_mask.astype(jnp.float32))).astype(jnp.bfloat16)
    cycle_coeff = (temper * jax.nn.sigmoid(cycle_logits)).astype(jnp.bfloat16)
    pod_coeff = (temper * jax.nn.sigmoid(pod_logits)).astype(jnp.bfloat16)
    image_grad = jnp.dot(own_coeff, own_text, preferred_element_type=jnp.float32)
    image_grad = image_grad + jnp.dot(cycle_coeff, cycle_text, preferred_element_type=jnp.float32)
    image_grad = image_grad + jnp.dot(pod_coeff, pod_text, preferred_element_type=jnp.float32)
    own_part = jnp.dot(own_coeff.T, image_rows, preferred_element_type=jnp.float32).astype(jnp.bfloat16)
    cycle_part = jnp.dot(cycle_coeff.T, image_rows, preferred_element_type=jnp.float32).astype(jnp.bfloat16)
    pod_part = jnp.dot(pod_coeff.T, image_rows, preferred_element_type=jnp.float32).astype(jnp.bfloat16)
    return row_loss, image_grad.astype(jnp.bfloat16), own_part, cycle_part, pod_part


def reference(images, texts, positive_index, log_scale, bias):
    width = images.shape[1]
    image_blocks = images.reshape(N_DP, N_OUTER, B, width)
    text_blocks = texts.reshape(N_DP, N_OUTER, B, width)
    cycle_blocks = jnp.roll(text_blocks, 1, axis=0)
    pod_blocks = jnp.roll(text_blocks, 1, axis=1)
    temper = jnp.exp(log_scale[0])
    offset_b = bias[0]

    def one_block(index):
        return block_terms((image_blocks.reshape(N_DP * N_OUTER, B, width)[index],
                            text_blocks.reshape(N_DP * N_OUTER, B, width)[index],
                            cycle_blocks.reshape(N_DP * N_OUTER, B, width)[index],
                            pod_blocks.reshape(N_DP * N_OUTER, B, width)[index],
                            positive_index[index], temper, offset_b))

    row_loss, image_grad, own_part, cycle_part, pod_part = lax.map(one_block, jnp.arange(N_DP * N_OUTER, dtype=jnp.int32))
    own_part = own_part.reshape(N_DP, N_OUTER, B, width).astype(jnp.float32)
    cycle_part = jnp.roll(cycle_part.reshape(N_DP, N_OUTER, B, width), -1, axis=0).astype(jnp.float32)
    pod_part = jnp.roll(pod_part.reshape(N_DP, N_OUTER, B, width), -1, axis=1).astype(jnp.float32)
    text_grad = (own_part + cycle_part + pod_part).astype(jnp.bfloat16)
    return (row_loss.reshape(N_DP * N_OUTER * B),
            image_grad.reshape(N_DP * N_OUTER * B, width),
            text_grad.reshape(N_DP * N_OUTER * B, width))
```

```python
import jax
import jax.numpy as jnp
from jax import lax
from jax.sharding import PartitionSpec as P


def passed_along(x, axis, by):
    devices = lax.axis_size(axis)
    return lax.ppermute(x, axis, [(i, (i + by) % devices) for i in range(devices)])


def logit_tile(left, right, temper, offset_b):
    product = lax.dot_general(
        left, right, (((1,), (1,)), ((), ())), preferred_element_type=jnp.float32
    )
    return temper * product + offset_b


def text_part(coeff, image_rows):
    product = lax.dot_general(
        coeff, image_rows, (((0,), (0,)), ((), ())), preferred_element_type=jnp.float32
    )
    return product.astype(jnp.bfloat16).astype(jnp.float32)


def far_text_part(images, texts, temper, offset_b):
    logits = logit_tile(images, texts, temper, offset_b)
    coeff = (temper * jax.nn.sigmoid(logits)).astype(jnp.bfloat16)
    return text_part(coeff, images)


def near_terms(images, texts, temper, offset_b):
    logits = logit_tile(images, texts, temper, offset_b)
    loss = jnp.sum(jax.nn.softplus(logits), axis=1)
    coeff = (temper * jax.nn.sigmoid(logits)).astype(jnp.bfloat16)
    return loss, jnp.dot(coeff, texts, preferred_element_type=jnp.float32)


def local(images, texts, positive_index, log_scale, bias):
    temper = jnp.exp(log_scale[0])
    offset_b = bias[0]
    row_count = images.shape[0]
    cycle_text = passed_along(texts, "dp", 1)
    cycle_images = passed_along(images, "dp", -1)
    pod_text = passed_along(texts, "outer", 1)
    pod_images = passed_along(images, "outer", -1)

    positive_mask = positive_index[0][:, None] == lax.broadcasted_iota(
        jnp.int32, (row_count, row_count), 1
    )
    own_logits = logit_tile(images, texts, temper, offset_b)
    signed = jnp.where(positive_mask, own_logits, -own_logits)
    loss_sum = jnp.sum(jax.nn.softplus(-signed), axis=1)
    own_coeff = (temper * (jax.nn.sigmoid(own_logits) - positive_mask.astype(jnp.float32))).astype(
        jnp.bfloat16
    )
    image_grad = jnp.dot(own_coeff, texts, preferred_element_type=jnp.float32)
    text_grad = text_part(own_coeff, images)

    pod_loss, pod_grad = near_terms(images, pod_text, temper, offset_b)
    text_grad = text_grad + far_text_part(pod_images, texts, temper, offset_b)
    cycle_loss, cycle_grad = near_terms(images, cycle_text, temper, offset_b)
    text_grad = text_grad + far_text_part(cycle_images, texts, temper, offset_b)
    row_loss = (loss_sum + pod_loss + cycle_loss) / (3.0 * row_count)
    image_grad = image_grad + pod_grad + cycle_grad
    return (row_loss, image_grad.astype(jnp.bfloat16), text_grad.astype(jnp.bfloat16))


def solution(mesh):
    in_specs = (
        P(("dp", "outer"), None),
        P(("dp", "outer"), None),
        P(("dp", "outer"), None),
        P(),
        P(),
    )
    out_specs = (P(("dp", "outer")), P(("dp", "outer"), None), P(("dp", "outer"), None))
    return jax.shard_map(local, mesh=mesh, in_specs=in_specs, out_specs=out_specs, check_vma=False)
```

```python
import jax
import jax.numpy as jnp
from jax import lax
from jax.experimental import pallas as pl
from jax.experimental.pallas import tpu as pltpu
from jax.sharding import PartitionSpec as P

VMEM = pl.BlockSpec(memory_space=pltpu.VMEM)
SMEM = pl.BlockSpec(memory_space=pltpu.SMEM)
F32 = jnp.float32
BF16 = jnp.bfloat16


def passed_along(x, axis, by):
    devices = lax.axis_size(axis)
    return lax.ppermute(x, axis, [(i, (i + by) % devices) for i in range(devices)])


def nt(left, right):
    return lax.dot_general(left, right, (((1,), (1,)), ((), ())), preferred_element_type=F32)


def tn(left, right):
    return lax.dot_general(left, right, (((0,), (0,)), ((), ())), preferred_element_type=F32)


def nn(left, right):
    return lax.dot_general(left, right, (((1,), (0,)), ((), ())), preferred_element_type=F32)


def tile_logits(scal, texts, images):
    return scal[0] * nt(texts, images) + scal[1]


def small(logits):
    return jnp.exp(-jnp.abs(logits))


def sigmoid(logits, e):
    return jnp.where(logits >= 0.0, 1.0, e) / (1.0 + e)


def softplus(v, e):
    return jnp.maximum(v, 0.0) + jnp.log1p(e)


def negative_tile(scal, texts, images, with_loss):
    logits = tile_logits(scal, texts, images)
    e = small(logits)
    coeff = (scal[0] * sigmoid(logits, e)).astype(BF16)
    if not with_loss:
        return coeff
    return coeff, jnp.sum(softplus(logits, e), axis=0, keepdims=True)


def own_kernel(scal, pos_ref, images_ref, texts_ref, loss_ref, igrad_ref, tgrad_ref):
    images, texts = images_ref[...], texts_ref[...]
    logits = tile_logits(scal, texts, images)
    mask = pos_ref[...] == lax.broadcasted_iota(jnp.int32, logits.shape, 0)
    e = small(logits)
    loss_ref[...] = jnp.sum(
        softplus(jnp.where(mask, -logits, logits), e), axis=0, keepdims=True
    )
    coeff = (scal[0] * (sigmoid(logits, e) - jnp.where(mask, 1.0, 0.0))).astype(BF16)
    igrad_ref[...] = tn(coeff, texts)
    tgrad_ref[...] = nn(coeff, images)


def middle_kernel(
    scal, images_ref, texts_ref, far_texts_ref, far_images_ref, loss_in, igrad_in, tgrad_in,
    loss_ref, igrad_ref, tgrad_ref,
):
    far_texts, far_images = far_texts_ref[...], far_images_ref[...]
    coeff, loss = negative_tile(scal, far_texts, images_ref[...], True)
    loss_ref[...] = loss_in[...] + loss
    igrad_ref[...] = igrad_in[...] + tn(coeff, far_texts)
    coeff = negative_tile(scal, texts_ref[...], far_images, False)
    tgrad_ref[...] = tgrad_in[...] + nn(coeff, far_images)


def last_image_kernel(scal, images_ref, far_texts_ref, loss_in, igrad_in, loss_ref, igrad_ref):
    far_texts = far_texts_ref[...]
    coeff, loss = negative_tile(scal, far_texts, images_ref[...], True)
    loss_ref[...] = loss_in[...] + loss
    igrad_ref[...] = (igrad_in[...] + tn(coeff, far_texts)).astype(BF16)


def last_text_kernel(scal, texts_ref, far_images_ref, loss_in, tgrad_in, loss_ref, tgrad_ref):
    loss_ref[...] = loss_in[...] / (3.0 * loss_in.shape[1])
    far_images = far_images_ref[...]
    coeff = negative_tile(scal, texts_ref[...], far_images, False)
    tgrad_ref[...] = (tgrad_in[...] + nn(coeff, far_images)).astype(BF16)


def call(kernel, outs, *args):
    return pl.pallas_call(
        kernel,
        out_shape=outs,
        in_specs=[SMEM] + [VMEM] * (len(args) - 1),
        out_specs=[VMEM] * len(outs),
        compiler_params=pltpu.CompilerParams(vmem_limit_bytes=40 * 1024 * 1024),
        cost_estimate=pl.CostEstimate(flops=1000, bytes_accessed=1000, transcendentals=0),
    )(*args)


def local(images, texts, positive_index, log_scale, bias):
    rows, width = images.shape
    cut = rows // 2
    scal = jnp.concatenate([jnp.exp(log_scale), bias])
    cycle_text = passed_along(texts, "dp", 1)
    cycle_images = passed_along(images, "dp", -1)
    pod_text = [passed_along(t, "outer", 1) for t in (texts[:cut], texts[cut:])]
    pod_images = [passed_along(i, "outer", -1) for i in (images[:cut], images[cut:])]

    loss_shape = jax.ShapeDtypeStruct((1, rows), F32)
    wide = jax.ShapeDtypeStruct((rows, width), F32)
    narrow = jax.ShapeDtypeStruct((rows, width), BF16)
    sums = call(own_kernel, [loss_shape, wide, wide], scal, positive_index, images, texts)
    for far in zip(pod_text, pod_images):
        sums = call(middle_kernel, [loss_shape, wide, wide], scal, images, texts, *far, *sums)
    loss, igrad, tgrad = sums
    loss, igrad = call(
        last_image_kernel, [loss_shape, narrow], scal, images, cycle_text, loss, igrad
    )
    loss, tgrad = call(
        last_text_kernel, [loss_shape, narrow], scal, texts, cycle_images, loss, tgrad
    )
    return loss.reshape(rows), igrad, tgrad


def solution(mesh):
    in_specs = (
        P(("dp", "outer"), None),
        P(("dp", "outer"), None),
        P(("dp", "outer"), None),
        P(),
        P(),
    )
    out_specs = (P(("dp", "outer")), P(("dp", "outer"), None), P(("dp", "outer"), None))
    return jax.shard_map(local, mesh=mesh, in_specs=in_specs, out_specs=out_specs, check_vma=False)
```

```python
import jax
import jax.numpy as jnp
from jax import lax
from jax.experimental import pallas as pl
from jax.experimental.pallas import tpu as pltpu
from jax.sharding import PartitionSpec as P

VMEM = pl.BlockSpec(memory_space=pltpu.VMEM)
SMEM = pl.BlockSpec(memory_space=pltpu.SMEM)
F32 = jnp.float32
BF16 = jnp.bfloat16


def passed_along(x, axis, by):
    devices = lax.axis_size(axis)
    return lax.ppermute(x, axis, [(i, (i + by) % devices) for i in range(devices)])


def nt(left, right):
    return lax.dot_general(left, right, (((1,), (1,)), ((), ())), preferred_element_type=F32)


def tn(left, right):
    return lax.dot_general(left, right, (((0,), (0,)), ((), ())), preferred_element_type=F32)


def nn(left, right):
    return lax.dot_general(left, right, (((1,), (0,)), ((), ())), preferred_element_type=F32)


def tile_logits(scal, texts, images):
    return scal[0] * nt(texts, images) + scal[1]


def small(logits):
    return jnp.exp(-jnp.abs(logits))


def sigmoid(logits, e):
    return jnp.where(logits >= 0.0, 1.0, e) / (1.0 + e)


def softplus(v, e):
    return jnp.maximum(v, 0.0) + jnp.log1p(e)


def image_side(scal, images, far_texts):
    logits = tile_logits(scal, far_texts, images)
    e = small(logits)
    coeff = (scal[0] * sigmoid(logits, e)).astype(BF16)
    return jnp.sum(softplus(logits, e), axis=0, keepdims=True), tn(coeff, far_texts)


def text_side(scal, texts, far_images):
    logits = tile_logits(scal, texts, far_images)
    coeff = (scal[0] * sigmoid(logits, small(logits))).astype(BF16)
    return nn(coeff, far_images)


def own_kernel(scal, pos_ref, images_ref, texts_ref, loss_ref, igrad_ref, tgrad_ref):
    images, texts = images_ref[...], texts_ref[...]
    logits = tile_logits(scal, texts, images)
    mask = pos_ref[...] == lax.broadcasted_iota(jnp.int32, logits.shape, 0)
    e = small(logits)
    loss_ref[...] = jnp.sum(
        softplus(jnp.where(mask, -logits, logits), e), axis=0, keepdims=True
    )
    coeff = (scal[0] * (sigmoid(logits, e) - jnp.where(mask, 1.0, 0.0))).astype(BF16)
    igrad_ref[...] = tn(coeff, texts)
    tgrad_ref[...] = nn(coeff, images)


def outer_kernel(
    scal, flags, images_ref, texts_ref, far_texts_ref, far_images_ref, loss_in, igrad_in, tgrad_in,
    loss_ref, igrad_ref, tgrad_ref,
):
    loss_ref[...] = loss_in[...]
    igrad_ref[...] = igrad_in[...]
    tgrad_ref[...] = tgrad_in[...]

    @pl.when(flags[0] == 0)
    def _():
        loss, grad = image_side(scal, images_ref[...], far_texts_ref[...])
        loss_ref[...] += loss
        igrad_ref[...] += grad

    @pl.when(flags[1] == 0)
    def _():
        tgrad_ref[...] += text_side(scal, texts_ref[...], far_images_ref[...])


def dp_image_kernel(
    scal, images_ref, far_texts_ref, loss_in, igrad_in, loss_ref, igrad_ref
):
    loss, grad = image_side(scal, images_ref[...], far_texts_ref[...])
    loss_ref[...] = loss_in[...] + loss
    igrad_ref[...] = igrad_in[...] + grad


def dp_text_kernel(scal, texts_ref, far_images_ref, loss_in, tgrad_in, loss_ref, tgrad_ref):
    loss_ref[...] = loss_in[...]
    tgrad_ref[...] = tgrad_in[...] + text_side(scal, texts_ref[...], far_images_ref[...])


def last_kernel(
    scal, flags, images_ref, texts_ref, cross_ref, loss_in, igrad_in, tgrad_in,
    loss_ref, igrad_ref, tgrad_ref,
):
    count = 3.0 * loss_in.shape[1]

    @pl.when(flags[0] == 0)
    def _():
        loss_ref[...] = loss_in[...] / count
        igrad_ref[...] = igrad_in[...].astype(BF16)

    @pl.when(flags[0] != 0)
    def _():
        loss, grad = image_side(scal, images_ref[...], cross_ref[...])
        loss_ref[...] = (loss_in[...] + loss) / count
        igrad_ref[...] = (igrad_in[...] + grad).astype(BF16)

    @pl.when(flags[1] == 0)
    def _():
        tgrad_ref[...] = tgrad_in[...].astype(BF16)

    @pl.when(flags[1] != 0)
    def _():
        tgrad_ref[...] = (
            tgrad_in[...] + text_side(scal, texts_ref[...], cross_ref[...])
        ).astype(BF16)


def call(kernel, outs, scalars, *args):
    return pl.pallas_call(
        kernel,
        out_shape=outs,
        in_specs=[SMEM] * len(scalars) + [VMEM] * len(args),
        out_specs=[VMEM] * len(outs),
        compiler_params=pltpu.CompilerParams(vmem_limit_bytes=40 * 1024 * 1024),
        cost_estimate=pl.CostEstimate(flops=1000, bytes_accessed=1000, transcendentals=0),
    )(*scalars, *args)


ROW = 8


def local(images, texts, positive_index, log_scale, bias):
    rows, width = images.shape
    outer = lax.axis_size("outer")
    here = lax.axis_index("outer")
    scal = jnp.concatenate([jnp.exp(log_scale), bias])
    first, last = here % ROW == 0, here % ROW == ROW - 1
    flags = jnp.stack([first, last]).astype(jnp.int32)

    def step(x, pairs):
        return lax.ppermute(x, "outer", pairs)

    ahead = [(o, (o + 1) % outer) for o in range(outer)]
    crossing = [(a, b) for a, b in ahead if b % ROW == 0]
    within = [(a, b) for a, b in ahead if b % ROW != 0]
    cycle_text = passed_along(texts, "dp", 1)
    cycle_images = passed_along(images, "dp", -1)
    cross = step(jnp.where(first, images, texts), crossing + [(b, a) for a, b in crossing])
    pod_text = step(texts, within)
    pod_images = step(images, [(b, a) for a, b in within])

    loss_shape = jax.ShapeDtypeStruct((1, rows), F32)
    wide = jax.ShapeDtypeStruct((rows, width), F32)
    narrow = jax.ShapeDtypeStruct((rows, width), BF16)
    loss, igrad, tgrad = call(
        own_kernel, [loss_shape, wide, wide], [scal], positive_index, images, texts
    )
    loss, igrad, tgrad = call(
        outer_kernel, [loss_shape, wide, wide], [scal, flags],
        images, texts, pod_text, pod_images, loss, igrad, tgrad,
    )
    loss, igrad = call(
        dp_image_kernel, [loss_shape, wide], [scal], images, cycle_text, loss, igrad
    )
    loss, tgrad = call(
        dp_text_kernel, [loss_shape, wide], [scal], texts, cycle_images, loss, tgrad
    )
    loss, igrad, tgrad = call(
        last_kernel, [loss_shape, narrow, narrow], [scal, flags],
        images, texts, cross, loss, igrad, tgrad,
    )
    return loss.reshape(rows), igrad, tgrad


def solution(mesh):
    in_specs = (
        P(("dp", "outer"), None),
        P(("dp", "outer"), None),
        P(("dp", "outer"), None),
        P(),
        P(),
    )
    out_specs = (P(("dp", "outer")), P(("dp", "outer"), None), P(("dp", "outer"), None))
    return jax.shard_map(local, mesh=mesh, in_specs=in_specs, out_specs=out_specs, check_vma=False)
```

```python
import jax
import jax.numpy as jnp
from jax import lax
from jax.experimental import pallas as pl
from jax.experimental.pallas import tpu as pltpu
from jax.sharding import PartitionSpec as P

VMEM = pl.BlockSpec(memory_space=pltpu.VMEM)
SMEM = pl.BlockSpec(memory_space=pltpu.SMEM)
F32 = jnp.float32
BF16 = jnp.bfloat16


def passed_along(x, axis, by):
    devices = lax.axis_size(axis)
    return lax.ppermute(x, axis, [(i, (i + by) % devices) for i in range(devices)])


def nt(left, right):
    return lax.dot_general(left, right, (((1,), (1,)), ((), ())), preferred_element_type=F32)


def tn(left, right):
    return lax.dot_general(left, right, (((0,), (0,)), ((), ())), preferred_element_type=F32)


def nn(left, right):
    return lax.dot_general(left, right, (((1,), (0,)), ((), ())), preferred_element_type=F32)


def tile_logits(scal, texts, images):
    return scal[0] * nt(texts, images) + scal[1]


def small(logits):
    return jnp.exp(-jnp.abs(logits))


def sigmoid(logits, e):
    return jnp.where(logits >= 0.0, 1.0, e) / (1.0 + e)


def softplus(v, e):
    return jnp.maximum(v, 0.0) + jnp.log1p(e)


def image_side(scal, images, far_texts):
    logits = tile_logits(scal, far_texts, images)
    e = small(logits)
    coeff = (scal[0] * sigmoid(logits, e)).astype(BF16)
    return jnp.sum(softplus(logits, e), axis=0, keepdims=True), tn(coeff, far_texts)


def text_side(scal, texts, far_images):
    logits = tile_logits(scal, texts, far_images)
    coeff = (scal[0] * sigmoid(logits, small(logits))).astype(BF16)
    return nn(coeff, far_images)


def own_kernel(scal, pos_ref, images_ref, texts_ref, loss_ref, igrad_ref, tgrad_ref):
    images, texts = images_ref[...], texts_ref[...]
    logits = tile_logits(scal, texts, images)
    mask = pos_ref[...] == lax.broadcasted_iota(jnp.int32, logits.shape, 0)
    e = small(logits)
    loss_ref[...] = jnp.sum(
        softplus(jnp.where(mask, -logits, logits), e), axis=0, keepdims=True
    )
    coeff = (scal[0] * (sigmoid(logits, e) - jnp.where(mask, 1.0, 0.0))).astype(BF16)
    igrad_ref[...] = tn(coeff, texts)
    tgrad_ref[...] = nn(coeff, images)


def outer_kernel(
    scal, flags, images_ref, texts_ref, far_texts_ref, far_images_ref, loss_in, igrad_in, tgrad_in,
    loss_ref, igrad_ref, tgrad_ref,
):
    loss_ref[...] = loss_in[...]
    igrad_ref[...] = igrad_in[...]
    tgrad_ref[...] = tgrad_in[...]

    @pl.when(flags[0] == 0)
    def _():
        loss, grad = image_side(scal, images_ref[...], far_texts_ref[...])
        loss_ref[...] += loss
        igrad_ref[...] += grad

    @pl.when(flags[1] == 0)
    def _():
        tgrad_ref[...] += text_side(scal, texts_ref[...], far_images_ref[...])


def dp_kernel(
    scal, images_ref, texts_ref, far_texts_ref, far_images_ref, loss_in, igrad_in, tgrad_in,
    loss_ref, igrad_ref, tgrad_ref,
):
    loss, grad = image_side(scal, images_ref[...], far_texts_ref[...])
    loss_ref[...] = loss_in[...] + loss
    igrad_ref[...] = igrad_in[...] + grad
    tgrad_ref[...] = tgrad_in[...] + text_side(scal, texts_ref[...], far_images_ref[...])


def last_kernel(
    scal, flags, images_ref, texts_ref, cross_ref, loss_in, igrad_in, tgrad_in,
    loss_ref, igrad_out, tgrad_out, igrad_ref, tgrad_ref, sems,
):
    count = 3.0 * loss_in.shape[1]

    @pl.when(flags[0] == 0)
    def _():
        loss_ref[...] = loss_in[...] / count
        igrad_ref[...] = igrad_in[...].astype(BF16)

    @pl.when(flags[0] != 0)
    def _():
        loss, grad = image_side(scal, images_ref[...], cross_ref[...])
        loss_ref[...] = (loss_in[...] + loss) / count
        igrad_ref[...] = (igrad_in[...] + grad).astype(BF16)

    image_copy = pltpu.make_async_copy(igrad_ref, igrad_out, sems.at[0])
    image_copy.start()

    @pl.when(flags[1] == 0)
    def _():
        tgrad_ref[...] = tgrad_in[...].astype(BF16)

    @pl.when(flags[1] != 0)
    def _():
        tgrad_ref[...] = (
            tgrad_in[...] + text_side(scal, texts_ref[...], cross_ref[...])
        ).astype(BF16)

    text_copy = pltpu.make_async_copy(tgrad_ref, tgrad_out, sems.at[1])
    text_copy.start()
    image_copy.wait()
    text_copy.wait()


def call(kernel, outs, scalars, *args, out_specs=None, scratch=()):
    return pl.pallas_call(
        kernel,
        out_shape=outs,
        in_specs=[SMEM] * len(scalars) + [VMEM] * len(args),
        out_specs=out_specs or [VMEM] * len(outs),
        scratch_shapes=scratch,
        compiler_params=pltpu.CompilerParams(vmem_limit_bytes=40 * 1024 * 1024),
        cost_estimate=pl.CostEstimate(flops=1000, bytes_accessed=1000, transcendentals=0),
    )(*scalars, *args)


ROW = 8


def local(images, texts, positive_index, log_scale, bias):
    rows, width = images.shape
    outer = lax.axis_size("outer")
    here = lax.axis_index("outer")
    scal = jnp.concatenate([jnp.exp(log_scale), bias])
    first, last = here % ROW == 0, here % ROW == ROW - 1
    flags = jnp.stack([first, last]).astype(jnp.int32)

    def step(x, pairs):
        return lax.ppermute(x, "outer", pairs)

    ahead = [(o, (o + 1) % outer) for o in range(outer)]
    crossing = [(a, b) for a, b in ahead if b % ROW == 0]
    within = [(a, b) for a, b in ahead if b % ROW != 0]
    cycle_text = passed_along(texts, "dp", 1)
    cycle_images = passed_along(images, "dp", -1)
    back = [(b, a) for a, b in within]
    cut = rows // 2
    cross = step(jnp.where(first, images, texts), crossing + [(b, a) for a, b in crossing])
    pod_texts = [step(t, within) for t in (texts[:cut], texts[cut:])]
    pod_images = [step(i, back) for i in (images[:cut], images[cut:])]

    loss_shape = jax.ShapeDtypeStruct((1, rows), F32)
    wide = jax.ShapeDtypeStruct((rows, width), F32)
    narrow = jax.ShapeDtypeStruct((rows, width), BF16)
    loss, igrad, tgrad = call(
        own_kernel, [loss_shape, wide, wide], [scal], positive_index, images, texts
    )
    for far in zip(pod_texts, pod_images):
        loss, igrad, tgrad = call(
            outer_kernel, [loss_shape, wide, wide], [scal, flags],
            images, texts, *far, loss, igrad, tgrad,
        )
    loss, igrad, tgrad = call(
        dp_kernel, [loss_shape, wide, wide], [scal],
        images, texts, cycle_text, cycle_images, loss, igrad, tgrad,
    )
    away = pl.BlockSpec(memory_space=pl.ANY)
    held = pltpu.VMEM((rows, width), BF16)
    loss, igrad, tgrad = call(
        last_kernel, [loss_shape, narrow, narrow], [scal, flags],
        images, texts, cross, loss, igrad, tgrad,
        out_specs=[VMEM, away, away],
        scratch=[held, held, pltpu.SemaphoreType.DMA((2,))],
    )
    return loss.reshape(rows), igrad, tgrad


def solution(mesh):
    in_specs = (
        P(("dp", "outer"), None),
        P(("dp", "outer"), None),
        P(("dp", "outer"), None),
        P(),
        P(),
    )
    out_specs = (P(("dp", "outer")), P(("dp", "outer"), None), P(("dp", "outer"), None))
    return jax.shard_map(local, mesh=mesh, in_specs=in_specs, out_specs=out_specs, check_vma=False)
```

```python
import jax
import jax.numpy as jnp
from jax import lax
from jax.experimental import pallas as pl
from jax.experimental.pallas import tpu as pltpu
from jax.sharding import PartitionSpec as P

VMEM = pl.BlockSpec(memory_space=pltpu.VMEM)
SMEM = pl.BlockSpec(memory_space=pltpu.SMEM)
F32 = jnp.float32
BF16 = jnp.bfloat16


def passed_along(x, axis, by):
    devices = lax.axis_size(axis)
    return lax.ppermute(x, axis, [(i, (i + by) % devices) for i in range(devices)])


def nt(left, right):
    return lax.dot_general(left, right, (((1,), (1,)), ((), ())), preferred_element_type=F32)


def tn(left, right):
    return lax.dot_general(left, right, (((0,), (0,)), ((), ())), preferred_element_type=F32)


def nn(left, right):
    return lax.dot_general(left, right, (((1,), (0,)), ((), ())), preferred_element_type=F32)


def tile_logits(scal, texts, images):
    return scal[0] * nt(texts, images) + scal[1]


def small(logits):
    return jnp.exp(-jnp.abs(logits))


def sigmoid(logits, e):
    return jnp.where(logits >= 0.0, 1.0, e) / (1.0 + e)


def softplus(v, e):
    return jnp.maximum(v, 0.0) + jnp.log1p(e)


def image_side(scal, images, far_texts):
    logits = tile_logits(scal, far_texts, images)
    e = small(logits)
    coeff = (scal[0] * sigmoid(logits, e)).astype(BF16)
    return jnp.sum(softplus(logits, e), axis=0, keepdims=True), tn(coeff, far_texts)


def text_side(scal, texts, far_images):
    logits = tile_logits(scal, texts, far_images)
    coeff = (scal[0] * sigmoid(logits, small(logits))).astype(BF16)
    return nn(coeff, far_images)


def own_kernel(
    scal, flags, pos_ref, images_ref, texts_ref, cross_texts_ref, cross_images_ref,
    loss_ref, igrad_ref, tgrad_ref,
):
    images, texts = images_ref[...], texts_ref[...]
    logits = tile_logits(scal, texts, images)
    mask = pos_ref[...] == lax.broadcasted_iota(jnp.int32, logits.shape, 0)
    e = small(logits)
    loss_ref[...] = jnp.sum(
        softplus(jnp.where(mask, -logits, logits), e), axis=0, keepdims=True
    )
    coeff = (scal[0] * (sigmoid(logits, e) - jnp.where(mask, 1.0, 0.0))).astype(BF16)
    igrad_ref[...] = tn(coeff, texts)
    tgrad_ref[...] = nn(coeff, images)

    @pl.when(flags[0] != 0)
    def _():
        loss, grad = image_side(scal, images_ref[...], cross_texts_ref[...])
        loss_ref[...] += loss
        igrad_ref[...] += grad

    @pl.when(flags[1] != 0)
    def _():
        tgrad_ref[...] += text_side(scal, texts_ref[...], cross_images_ref[...])


def outer_kernel(
    scal, flags, images_ref, texts_ref, far_texts_ref, far_images_ref, loss_in, igrad_in, tgrad_in,
    loss_ref, igrad_ref, tgrad_ref,
):
    loss_ref[...] = loss_in[...]
    igrad_ref[...] = igrad_in[...]
    tgrad_ref[...] = tgrad_in[...]

    @pl.when(flags[0] == 0)
    def _():
        loss, grad = image_side(scal, images_ref[...], far_texts_ref[...])
        loss_ref[...] += loss
        igrad_ref[...] += grad

    @pl.when(flags[1] == 0)
    def _():
        tgrad_ref[...] += text_side(scal, texts_ref[...], far_images_ref[...])


def last_kernel(
    scal, images_ref, texts_ref, far_texts_ref, far_images_ref, loss_in, igrad_in, tgrad_in,
    loss_ref, igrad_out, tgrad_out, igrad_ref, tgrad_ref, sems,
):
    loss, grad = image_side(scal, images_ref[...], far_texts_ref[...])
    loss_ref[...] = (loss_in[...] + loss) / (3.0 * loss_in.shape[1])
    igrad_ref[...] = (igrad_in[...] + grad).astype(BF16)
    image_copy = pltpu.make_async_copy(igrad_ref, igrad_out, sems.at[0])
    image_copy.start()
    grad = text_side(scal, texts_ref[...], far_images_ref[...])
    tgrad_ref[...] = (tgrad_in[...] + grad).astype(BF16)
    text_copy = pltpu.make_async_copy(tgrad_ref, tgrad_out, sems.at[1])
    text_copy.start()
    image_copy.wait()
    text_copy.wait()


def call(kernel, outs, scalars, *args, out_specs=None, scratch=()):
    return pl.pallas_call(
        kernel,
        out_shape=outs,
        in_specs=[SMEM] * len(scalars) + [VMEM] * len(args),
        out_specs=out_specs or [VMEM] * len(outs),
        scratch_shapes=scratch,
        compiler_params=pltpu.CompilerParams(vmem_limit_bytes=40 * 1024 * 1024),
        cost_estimate=pl.CostEstimate(flops=1000, bytes_accessed=1000, transcendentals=0),
    )(*scalars, *args)


ROW = 8


def local(images, texts, positive_index, log_scale, bias):
    rows, width = images.shape
    outer = lax.axis_size("outer")
    here = lax.axis_index("outer")
    scal = jnp.concatenate([jnp.exp(log_scale), bias])
    first, last = here % ROW == 0, here % ROW == ROW - 1
    flags = jnp.stack([first, last]).astype(jnp.int32)

    def step(x, pairs):
        return lax.ppermute(x, "outer", pairs)

    ahead = [(o, (o + 1) % outer) for o in range(outer)]
    crossing = [(a, b) for a, b in ahead if b % ROW == 0]
    within = [(a, b) for a, b in ahead if b % ROW != 0]
    turned = [(b, a) for a, b in crossing]
    back = [(b, a) for a, b in within]
    cross_texts = step(texts, crossing)
    cross_images = step(images, turned)
    cross_texts, cross_images, texts, images = lax.optimization_barrier(
        (cross_texts, cross_images, texts, images)
    )
    cycle_text = passed_along(texts, "dp", 1)
    cycle_images = passed_along(images, "dp", -1)
    cut = rows // 2
    pod_texts = [step(t, within) for t in (texts[:cut], texts[cut:])]
    pod_images = [step(i, back) for i in (images[:cut], images[cut:])]

    loss_shape = jax.ShapeDtypeStruct((1, rows), F32)
    wide = jax.ShapeDtypeStruct((rows, width), F32)
    narrow = jax.ShapeDtypeStruct((rows, width), BF16)
    sums = call(
        own_kernel, [loss_shape, wide, wide], [scal, flags],
        positive_index, images, texts, cross_texts, cross_images,
    )
    for far in zip(pod_texts, pod_images):
        sums = call(
            outer_kernel, [loss_shape, wide, wide], [scal, flags], images, texts, *far, *sums
        )
    away = pl.BlockSpec(memory_space=pl.ANY)
    held = pltpu.VMEM((rows, width), BF16)
    loss, igrad, tgrad = call(
        last_kernel, [loss_shape, narrow, narrow], [scal],
        images, texts, cycle_text, cycle_images, *sums,
        out_specs=[VMEM, away, away],
        scratch=[held, held, pltpu.SemaphoreType.DMA((2,))],
    )
    return loss.reshape(rows), igrad, tgrad


def solution(mesh):
    in_specs = (
        P(("dp", "outer"), None),
        P(("dp", "outer"), None),
        P(("dp", "outer"), None),
        P(),
        P(),
    )
    out_specs = (P(("dp", "outer")), P(("dp", "outer"), None), P(("dp", "outer"), None))
    return jax.shard_map(local, mesh=mesh, in_specs=in_specs, out_specs=out_specs, check_vma=False)
```

```python
import jax
import jax.numpy as jnp
from jax import lax
from jax.experimental import pallas as pl
from jax.experimental.pallas import tpu as pltpu
from jax.sharding import PartitionSpec as P

VMEM = pl.BlockSpec(memory_space=pltpu.VMEM)
SMEM = pl.BlockSpec(memory_space=pltpu.SMEM)
F32 = jnp.float32
BF16 = jnp.bfloat16


def passed_along(x, axis, by):
    devices = lax.axis_size(axis)
    return lax.ppermute(x, axis, [(i, (i + by) % devices) for i in range(devices)])


def nt(left, right):
    return lax.dot_general(left, right, (((1,), (1,)), ((), ())), preferred_element_type=F32)


def tn(left, right):
    return lax.dot_general(left, right, (((0,), (0,)), ((), ())), preferred_element_type=F32)


def nn(left, right):
    return lax.dot_general(left, right, (((1,), (0,)), ((), ())), preferred_element_type=F32)


def tile_logits(scal, texts, images):
    return scal[0] * nt(texts, images) + scal[1]


def small(logits):
    return jnp.exp(-jnp.abs(logits))


def sigmoid(logits, e):
    return jnp.where(logits >= 0.0, 1.0, e) / (1.0 + e)


def softplus(v, e):
    return jnp.maximum(v, 0.0) + jnp.log1p(e)


def image_side(scal, images, far_texts):
    logits = tile_logits(scal, far_texts, images)
    e = small(logits)
    coeff = (scal[0] * sigmoid(logits, e)).astype(BF16)
    return jnp.sum(softplus(logits, e), axis=0, keepdims=True), tn(coeff, far_texts)


def text_side(scal, texts, far_images):
    logits = tile_logits(scal, texts, far_images)
    coeff = (scal[0] * sigmoid(logits, small(logits))).astype(BF16)
    return nn(coeff, far_images)


def own_kernel(
    scal, flags, pos_ref, images_ref, texts_ref, cross_ref, loss_ref, igrad_ref, tgrad_ref
):
    images, texts = images_ref[...], texts_ref[...]
    logits = tile_logits(scal, texts, images)
    mask = pos_ref[...] == lax.broadcasted_iota(jnp.int32, logits.shape, 0)
    e = small(logits)
    loss_ref[...] = jnp.sum(
        softplus(jnp.where(mask, -logits, logits), e), axis=0, keepdims=True
    )
    coeff = (scal[0] * (sigmoid(logits, e) - jnp.where(mask, 1.0, 0.0))).astype(BF16)
    igrad_ref[...] = tn(coeff, texts)
    tgrad_ref[...] = nn(coeff, images)

    @pl.when(flags[0] != 0)
    def _():
        loss, grad = image_side(scal, images_ref[...], cross_ref[...])
        loss_ref[...] += loss
        igrad_ref[...] += grad

    @pl.when(flags[1] != 0)
    def _():
        tgrad_ref[...] += text_side(scal, texts_ref[...], cross_ref[...])


def outer_kernel(
    scal, flags, images_ref, texts_ref, far_texts_ref, far_images_ref, loss_in, igrad_in, tgrad_in,
    loss_ref, igrad_ref, tgrad_ref,
):
    loss_ref[...] = loss_in[...]
    igrad_ref[...] = igrad_in[...]
    tgrad_ref[...] = tgrad_in[...]

    @pl.when(flags[0] == 0)
    def _():
        loss, grad = image_side(scal, images_ref[...], far_texts_ref[...])
        loss_ref[...] += loss
        igrad_ref[...] += grad

    @pl.when(flags[1] == 0)
    def _():
        tgrad_ref[...] += text_side(scal, texts_ref[...], far_images_ref[...])


def last_kernel(
    scal, images_ref, texts_ref, far_texts_ref, far_images_ref, loss_in, igrad_in, tgrad_in,
    loss_ref, igrad_out, tgrad_out, igrad_ref, tgrad_ref, sems,
):
    loss, grad = image_side(scal, images_ref[...], far_texts_ref[...])
    loss_ref[...] = (loss_in[...] + loss) / (3.0 * loss_in.shape[1])
    igrad_ref[...] = (igrad_in[...] + grad).astype(BF16)
    image_copy = pltpu.make_async_copy(igrad_ref, igrad_out, sems.at[0])
    image_copy.start()
    grad = text_side(scal, texts_ref[...], far_images_ref[...])
    tgrad_ref[...] = (tgrad_in[...] + grad).astype(BF16)
    text_copy = pltpu.make_async_copy(tgrad_ref, tgrad_out, sems.at[1])
    text_copy.start()
    image_copy.wait()
    text_copy.wait()


def call(kernel, outs, scalars, *args, out_specs=None, scratch=()):
    return pl.pallas_call(
        kernel,
        out_shape=outs,
        in_specs=[SMEM] * len(scalars) + [VMEM] * len(args),
        out_specs=out_specs or [VMEM] * len(outs),
        scratch_shapes=scratch,
        compiler_params=pltpu.CompilerParams(vmem_limit_bytes=40 * 1024 * 1024),
        cost_estimate=pl.CostEstimate(flops=1000, bytes_accessed=1000, transcendentals=0),
    )(*scalars, *args)


ROW = 8


def local(images, texts, positive_index, log_scale, bias):
    rows, width = images.shape
    outer = lax.axis_size("outer")
    here = lax.axis_index("outer")
    scal = jnp.concatenate([jnp.exp(log_scale), bias])
    first, last = here % ROW == 0, here % ROW == ROW - 1
    flags = jnp.stack([first, last]).astype(jnp.int32)

    def step(x, pairs):
        return lax.ppermute(x, "outer", pairs)

    ahead = [(o, (o + 1) % outer) for o in range(outer)]
    crossing = [(a, b) for a, b in ahead if b % ROW == 0]
    within = [(a, b) for a, b in ahead if b % ROW != 0]
    back = [(b, a) for a, b in within]
    mixed, texts, images = lax.optimization_barrier(
        (jnp.where(first, images, texts), texts, images)
    )
    cross = step(mixed, crossing + [(b, a) for a, b in crossing])
    cycle_text = passed_along(texts, "dp", 1)
    cycle_images = passed_along(images, "dp", -1)
    pod_text = step(texts, within)
    pod_images = step(images, back)

    loss_shape = jax.ShapeDtypeStruct((1, rows), F32)
    wide = jax.ShapeDtypeStruct((rows, width), F32)
    narrow = jax.ShapeDtypeStruct((rows, width), BF16)
    sums = call(
        own_kernel, [loss_shape, wide, wide], [scal, flags],
        positive_index, images, texts, cross,
    )
    sums = call(
        outer_kernel, [loss_shape, wide, wide], [scal, flags],
        images, texts, pod_text, pod_images, *sums,
    )
    away = pl.BlockSpec(memory_space=pl.ANY)
    held = pltpu.VMEM((rows, width), BF16)
    loss, igrad, tgrad = call(
        last_kernel, [loss_shape, narrow, narrow], [scal],
        images, texts, cycle_text, cycle_images, *sums,
        out_specs=[VMEM, away, away],
        scratch=[held, held, pltpu.SemaphoreType.DMA((2,))],
    )
    return loss.reshape(rows), igrad, tgrad


def solution(mesh):
    in_specs = (
        P(("dp", "outer"), None),
        P(("dp", "outer"), None),
        P(("dp", "outer"), None),
        P(),
        P(),
    )
    out_specs = (P(("dp", "outer")), P(("dp", "outer"), None), P(("dp", "outer"), None))
    return jax.shard_map(local, mesh=mesh, in_specs=in_specs, out_specs=out_specs, check_vma=False)
```

```python
import jax
import jax.numpy as jnp
from jax import lax
from jax.experimental import pallas as pl
from jax.experimental.pallas import tpu as pltpu
from jax.sharding import PartitionSpec as P

VMEM = pl.BlockSpec(memory_space=pltpu.VMEM)
SMEM = pl.BlockSpec(memory_space=pltpu.SMEM)
F32 = jnp.float32
BF16 = jnp.bfloat16


def passed_along(x, axis, by):
    devices = lax.axis_size(axis)
    return lax.ppermute(x, axis, [(i, (i + by) % devices) for i in range(devices)])


def nt(left, right):
    return lax.dot_general(left, right, (((1,), (1,)), ((), ())), preferred_element_type=F32)


def tn(left, right):
    return lax.dot_general(left, right, (((0,), (0,)), ((), ())), preferred_element_type=F32)


def nn(left, right):
    return lax.dot_general(left, right, (((1,), (0,)), ((), ())), preferred_element_type=F32)


def tile_logits(scal, texts, images):
    return scal[0] * nt(texts, images) + scal[1]


def small(logits):
    return jnp.exp(-jnp.abs(logits))


def sigmoid(logits, e):
    return jnp.where(logits >= 0.0, 1.0, e) / (1.0 + e)


def softplus(v, e):
    return jnp.maximum(v, 0.0) + jnp.log1p(e)


def image_side(scal, images, far_texts):
    logits = tile_logits(scal, far_texts, images)
    e = small(logits)
    coeff = (scal[0] * sigmoid(logits, e)).astype(BF16)
    return jnp.sum(softplus(logits, e), axis=0, keepdims=True), tn(coeff, far_texts)


def text_side(scal, texts, far_images):
    logits = tile_logits(scal, texts, far_images)
    coeff = (scal[0] * sigmoid(logits, small(logits))).astype(BF16)
    return nn(coeff, far_images)


def own_kernel(scal, pos_ref, images_ref, texts_ref, loss_ref, igrad_ref, tgrad_ref):
    images, texts = images_ref[...], texts_ref[...]
    logits = tile_logits(scal, texts, images)
    mask = pos_ref[...] == lax.broadcasted_iota(jnp.int32, logits.shape, 0)
    e = small(logits)
    loss_ref[...] = jnp.sum(
        softplus(jnp.where(mask, -logits, logits), e), axis=0, keepdims=True
    )
    coeff = (scal[0] * (sigmoid(logits, e) - jnp.where(mask, 1.0, 0.0))).astype(BF16)
    igrad_ref[...] = tn(coeff, texts)
    tgrad_ref[...] = nn(coeff, images)


def outer_kernel(
    scal, images_ref, texts_ref, far_texts_ref, far_images_ref, loss_in, igrad_in, tgrad_in,
    loss_ref, igrad_ref, tgrad_ref,
):
    loss, grad = image_side(scal, images_ref[...], far_texts_ref[...])
    loss_ref[...] = loss_in[...] + loss
    igrad_ref[...] = igrad_in[...] + grad
    tgrad_ref[...] = tgrad_in[...] + text_side(scal, texts_ref[...], far_images_ref[...])


def last_kernel(
    scal, images_ref, texts_ref, far_texts_ref, far_images_ref, loss_in, igrad_in, tgrad_in,
    loss_ref, igrad_out, tgrad_out, igrad_ref, tgrad_ref, sems,
):
    loss, grad = image_side(scal, images_ref[...], far_texts_ref[...])
    loss_ref[...] = (loss_in[...] + loss) / (3.0 * loss_in.shape[1])
    igrad_ref[...] = (igrad_in[...] + grad).astype(BF16)
    image_copy = pltpu.make_async_copy(igrad_ref, igrad_out, sems.at[0])
    image_copy.start()
    grad = text_side(scal, texts_ref[...], far_images_ref[...])
    tgrad_ref[...] = (tgrad_in[...] + grad).astype(BF16)
    text_copy = pltpu.make_async_copy(tgrad_ref, tgrad_out, sems.at[1])
    text_copy.start()
    image_copy.wait()
    text_copy.wait()


def call(kernel, outs, scalars, *args, out_specs=None, scratch=()):
    return pl.pallas_call(
        kernel,
        out_shape=outs,
        in_specs=[SMEM] * len(scalars) + [VMEM] * len(args),
        out_specs=out_specs or [VMEM] * len(outs),
        scratch_shapes=scratch,
        compiler_params=pltpu.CompilerParams(vmem_limit_bytes=40 * 1024 * 1024),
        cost_estimate=pl.CostEstimate(flops=1000, bytes_accessed=1000, transcendentals=0),
    )(*scalars, *args)


def local(images, texts, positive_index, log_scale, bias):
    rows, width = images.shape
    scal = jnp.concatenate([jnp.exp(log_scale), bias])
    pod_text = passed_along(texts, "outer", 1)
    pod_images = passed_along(images, "outer", -1)
    cycle_text = passed_along(texts, "dp", 1)
    cycle_images = passed_along(images, "dp", -1)

    loss_shape = jax.ShapeDtypeStruct((1, rows), F32)
    wide = jax.ShapeDtypeStruct((rows, width), F32)
    narrow = jax.ShapeDtypeStruct((rows, width), BF16)
    sums = call(own_kernel, [loss_shape, wide, wide], [scal], positive_index, images, texts)
    sums = call(
        outer_kernel, [loss_shape, wide, wide], [scal], images, texts, pod_text, pod_images, *sums
    )
    away = pl.BlockSpec(memory_space=pl.ANY)
    held = pltpu.VMEM((rows, width), BF16)
    loss, igrad, tgrad = call(
        last_kernel, [loss_shape, narrow, narrow], [scal],
        images, texts, cycle_text, cycle_images, *sums,
        out_specs=[VMEM, away, away],
        scratch=[held, held, pltpu.SemaphoreType.DMA((2,))],
    )
    return loss.reshape(rows), igrad, tgrad


def solution(mesh):
    in_specs = (
        P(("dp", "outer"), None),
        P(("dp", "outer"), None),
        P(("dp", "outer"), None),
        P(),
        P(),
    )
    out_specs = (P(("dp", "outer")), P(("dp", "outer"), None), P(("dp", "outer"), None))
    return jax.shard_map(local, mesh=mesh, in_specs=in_specs, out_specs=out_specs, check_vma=False)
```

```python
import jax
import jax.numpy as jnp
from jax import lax
from jax.experimental import pallas as pl
from jax.experimental.pallas import tpu as pltpu
from jax.sharding import PartitionSpec as P

VMEM = pl.BlockSpec(memory_space=pltpu.VMEM)
SMEM = pl.BlockSpec(memory_space=pltpu.SMEM)
F32 = jnp.float32
BF16 = jnp.bfloat16


def passed_along(x, axis, by):
    devices = lax.axis_size(axis)
    return lax.ppermute(x, axis, [(i, (i + by) % devices) for i in range(devices)])


def nt(left, right):
    return lax.dot_general(left, right, (((1,), (1,)), ((), ())), preferred_element_type=F32)


def tn(left, right):
    return lax.dot_general(left, right, (((0,), (0,)), ((), ())), preferred_element_type=F32)


def nn(left, right):
    return lax.dot_general(left, right, (((1,), (0,)), ((), ())), preferred_element_type=F32)


def tile_logits(scal, texts, images):
    return scal[0] * nt(texts, images) + scal[1]


def small(logits):
    return jnp.exp(-jnp.abs(logits))


def sigmoid(logits, e):
    return jnp.where(logits >= 0.0, 1.0, e) / (1.0 + e)


def softplus(v, e):
    return jnp.maximum(v, 0.0) + jnp.log1p(e)


def image_side(scal, images, far_texts):
    logits = tile_logits(scal, far_texts, images)
    e = small(logits)
    coeff = (scal[0] * sigmoid(logits, e)).astype(BF16)
    return jnp.sum(softplus(logits, e), axis=0, keepdims=True), tn(coeff, far_texts)


def text_side(scal, texts, far_images):
    logits = tile_logits(scal, texts, far_images)
    coeff = (scal[0] * sigmoid(logits, small(logits))).astype(BF16)
    return nn(coeff, far_images)


def own_kernel(scal, pos_ref, images_ref, texts_ref, loss_ref, igrad_ref, tgrad_ref):
    images, texts = images_ref[...], texts_ref[...]
    logits = tile_logits(scal, texts, images)
    mask = pos_ref[...] == lax.broadcasted_iota(jnp.int32, logits.shape, 0)
    e = small(logits)
    loss_ref[...] = jnp.sum(
        softplus(jnp.where(mask, -logits, logits), e), axis=0, keepdims=True
    )
    coeff = (scal[0] * (sigmoid(logits, e) - jnp.where(mask, 1.0, 0.0))).astype(BF16)
    igrad_ref[...] = tn(coeff, texts)
    tgrad_ref[...] = nn(coeff, images)


def outer_text_kernel(scal, images_ref, far_texts_ref, loss_in, igrad_in, loss_ref, igrad_ref):
    loss, grad = image_side(scal, images_ref[...], far_texts_ref[...])
    loss_ref[...] = loss_in[...] + loss
    igrad_ref[...] = igrad_in[...] + grad


def middle_kernel(
    scal, images_ref, texts_ref, far_texts_ref, far_images_ref, loss_in, igrad_in, tgrad_in,
    loss_ref, igrad_out, tgrad_ref, igrad_ref, sem,
):
    loss, grad = image_side(scal, images_ref[...], far_texts_ref[...])
    loss_ref[...] = loss_in[...] + loss
    igrad_ref[...] = (igrad_in[...] + grad).astype(BF16)
    copy = pltpu.make_async_copy(igrad_ref, igrad_out, sem)
    copy.start()
    tgrad_ref[...] = tgrad_in[...] + text_side(scal, texts_ref[...], far_images_ref[...])
    copy.wait()


def last_kernel(scal, texts_ref, far_images_ref, loss_in, tgrad_in, loss_ref, tgrad_ref):
    loss_ref[...] = loss_in[...] / (3.0 * loss_in.shape[1])
    grad = text_side(scal, texts_ref[...], far_images_ref[...])
    tgrad_ref[...] = (tgrad_in[...] + grad).astype(BF16)


def call(kernel, outs, scalars, *args, out_specs=None, scratch=()):
    return pl.pallas_call(
        kernel,
        out_shape=outs,
        in_specs=[SMEM] * len(scalars) + [VMEM] * len(args),
        out_specs=out_specs or [VMEM] * len(outs),
        scratch_shapes=scratch,
        compiler_params=pltpu.CompilerParams(vmem_limit_bytes=40 * 1024 * 1024),
        cost_estimate=pl.CostEstimate(flops=1000, bytes_accessed=1000, transcendentals=0),
    )(*scalars, *args)


def local(images, texts, positive_index, log_scale, bias):
    rows, width = images.shape
    scal = jnp.concatenate([jnp.exp(log_scale), bias])
    pod_text = passed_along(texts, "outer", 1)
    pod_images = passed_along(images, "outer", -1)
    cycle_text = passed_along(texts, "dp", 1)
    cycle_images = passed_along(images, "dp", -1)

    loss_shape = jax.ShapeDtypeStruct((1, rows), F32)
    wide = jax.ShapeDtypeStruct((rows, width), F32)
    narrow = jax.ShapeDtypeStruct((rows, width), BF16)
    loss, igrad, tgrad = call(
        own_kernel, [loss_shape, wide, wide], [scal], positive_index, images, texts
    )
    loss, igrad = call(
        outer_text_kernel, [loss_shape, wide], [scal], images, pod_text, loss, igrad
    )
    loss, igrad, tgrad = call(
        middle_kernel, [loss_shape, narrow, wide], [scal],
        images, texts, cycle_text, pod_images, loss, igrad, tgrad,
        out_specs=[VMEM, pl.BlockSpec(memory_space=pl.ANY), VMEM],
        scratch=[pltpu.VMEM((rows, width), BF16), pltpu.SemaphoreType.DMA(())],
    )
    loss, tgrad = call(
        last_kernel, [loss_shape, narrow], [scal], texts, cycle_images, loss, tgrad
    )
    return loss.reshape(rows), igrad, tgrad


def solution(mesh):
    in_specs = (
        P(("dp", "outer"), None),
        P(("dp", "outer"), None),
        P(("dp", "outer"), None),
        P(),
        P(),
    )
    out_specs = (P(("dp", "outer")), P(("dp", "outer"), None), P(("dp", "outer"), None))
    return jax.shard_map(local, mesh=mesh, in_specs=in_specs, out_specs=out_specs, check_vma=False)
```

```python
import jax
import jax.numpy as jnp
from jax import lax
from jax.experimental import pallas as pl
from jax.experimental.pallas import tpu as pltpu
from jax.sharding import PartitionSpec as P

VMEM = pl.BlockSpec(memory_space=pltpu.VMEM)
SMEM = pl.BlockSpec(memory_space=pltpu.SMEM)
F32 = jnp.float32
BF16 = jnp.bfloat16


def passed_along(x, axis, by):
    devices = lax.axis_size(axis)
    return lax.ppermute(x, axis, [(i, (i + by) % devices) for i in range(devices)])


def nt(left, right):
    return lax.dot_general(left, right, (((1,), (1,)), ((), ())), preferred_element_type=F32)


def tn(left, right):
    return lax.dot_general(left, right, (((0,), (0,)), ((), ())), preferred_element_type=F32)


def nn(left, right):
    return lax.dot_general(left, right, (((1,), (0,)), ((), ())), preferred_element_type=F32)


def tile_logits(scal, texts, images):
    return scal[0] * nt(texts, images) + scal[1]


def small(logits):
    return jnp.exp(-jnp.abs(logits))


def sigmoid(logits, e):
    return jnp.where(logits >= 0.0, 1.0, e) / (1.0 + e)


def softplus(v, e):
    return jnp.maximum(v, 0.0) + jnp.log1p(e)


def image_side(scal, images, far_texts):
    logits = tile_logits(scal, far_texts, images)
    e = small(logits)
    coeff = (scal[0] * sigmoid(logits, e)).astype(BF16)
    return jnp.sum(softplus(logits, e), axis=0, keepdims=True), tn(coeff, far_texts)


def text_side(scal, texts, far_images):
    logits = tile_logits(scal, texts, far_images)
    coeff = (scal[0] * sigmoid(logits, small(logits))).astype(BF16)
    return nn(coeff, far_images)


def own_kernel(scal, pos_ref, images_ref, texts_ref, loss_ref, igrad_ref, tgrad_ref):
    images, texts = images_ref[...], texts_ref[...]
    logits = tile_logits(scal, texts, images)
    mask = pos_ref[...] == lax.broadcasted_iota(jnp.int32, logits.shape, 0)
    e = small(logits)
    loss_ref[...] = jnp.sum(
        softplus(jnp.where(mask, -logits, logits), e), axis=0, keepdims=True
    )
    coeff = (scal[0] * (sigmoid(logits, e) - jnp.where(mask, 1.0, 0.0))).astype(BF16)
    igrad_ref[...] = tn(coeff, texts)
    tgrad_ref[...] = nn(coeff, images)


def outer_kernel(
    scal, role, images_ref, texts_ref, pair_ref, loss_in, igrad_in, tgrad_in,
    loss_ref, igrad_ref, tgrad_ref,
):
    far_ref = pair_ref.at[role[1]]
    loss_ref[...] = loss_in[...]

    @pl.when(role[0] != 0)
    def _():
        loss, grad = image_side(scal, images_ref[...], far_ref[...])
        loss_ref[...] += loss
        igrad_ref[...] = igrad_in[...] + grad
        tgrad_ref[...] = tgrad_in[...]

    @pl.when(role[0] == 0)
    def _():
        igrad_ref[...] = igrad_in[...]
        tgrad_ref[...] = tgrad_in[...] + text_side(scal, texts_ref[...], far_ref[...])


def last_kernel(
    scal, images_ref, texts_ref, far_texts_ref, far_images_ref, loss_in, igrad_in, tgrad_in,
    loss_ref, igrad_out, tgrad_out, igrad_ref, tgrad_ref, sems,
):
    loss, grad = image_side(scal, images_ref[...], far_texts_ref[...])
    loss_ref[...] = (loss_in[...] + loss) / (3.0 * loss_in.shape[1])
    igrad_ref[...] = (igrad_in[...] + grad).astype(BF16)
    image_copy = pltpu.make_async_copy(igrad_ref, igrad_out, sems.at[0])
    image_copy.start()
    grad = text_side(scal, texts_ref[...], far_images_ref[...])
    tgrad_ref[...] = (tgrad_in[...] + grad).astype(BF16)
    text_copy = pltpu.make_async_copy(tgrad_ref, tgrad_out, sems.at[1])
    text_copy.start()
    image_copy.wait()
    text_copy.wait()


def call(kernel, outs, scalars, *args, out_specs=None, scratch=()):
    return pl.pallas_call(
        kernel,
        out_shape=outs,
        in_specs=[SMEM] * len(scalars) + [VMEM] * len(args),
        out_specs=out_specs or [VMEM] * len(outs),
        scratch_shapes=scratch,
        compiler_params=pltpu.CompilerParams(vmem_limit_bytes=40 * 1024 * 1024),
        cost_estimate=pl.CostEstimate(flops=1000, bytes_accessed=1000, transcendentals=0),
    )(*scalars, *args)


def local(images, texts, positive_index, log_scale, bias):
    rows, width = images.shape
    outer = lax.axis_size("outer")
    core = lax.axis_index("outer") % 2
    scal = jnp.concatenate([jnp.exp(log_scale), bias])
    cycle_text = passed_along(texts, "dp", 1)
    cycle_images = passed_along(images, "dp", -1)
    chips = [[o, o + 1] for o in range(0, outer, 2)]
    links = [[o, (o + 1) % outer] for o in range(1, outer, 2)]
    even = core == 0
    link_pair = lax.all_gather(
        jnp.where(even, images, texts), "outer", axis_index_groups=links
    )
    chip_pair = lax.all_gather(
        jnp.where(even, texts, images), "outer", axis_index_groups=chips
    )

    loss_shape = jax.ShapeDtypeStruct((1, rows), F32)
    wide = jax.ShapeDtypeStruct((rows, width), F32)
    narrow = jax.ShapeDtypeStruct((rows, width), BF16)
    sums = call(own_kernel, [loss_shape, wide, wide], [scal], positive_index, images, texts)
    for pair, role in ((chip_pair, [core, 1 - core]), (link_pair, [1 - core, core])):
        role = jnp.stack(role).astype(jnp.int32)
        sums = call(
            outer_kernel, [loss_shape, wide, wide], [scal, role], images, texts, pair, *sums
        )
    away = pl.BlockSpec(memory_space=pl.ANY)
    held = pltpu.VMEM((rows, width), BF16)
    loss, igrad, tgrad = call(
        last_kernel, [loss_shape, narrow, narrow], [scal],
        images, texts, cycle_text, cycle_images, *sums,
        out_specs=[VMEM, away, away],
        scratch=[held, held, pltpu.SemaphoreType.DMA((2,))],
    )
    return loss.reshape(rows), igrad, tgrad


def solution(mesh):
    in_specs = (
        P(("dp", "outer"), None),
        P(("dp", "outer"), None),
        P(("dp", "outer"), None),
        P(),
        P(),
    )
    out_specs = (P(("dp", "outer")), P(("dp", "outer"), None), P(("dp", "outer"), None))
    return jax.shard_map(local, mesh=mesh, in_specs=in_specs, out_specs=out_specs, check_vma=False)
```

```python
import jax
import jax.numpy as jnp
from jax import lax
from jax.experimental import pallas as pl
from jax.experimental.pallas import tpu as pltpu
from jax.sharding import PartitionSpec as P

VMEM = pl.BlockSpec(memory_space=pltpu.VMEM)
SMEM = pl.BlockSpec(memory_space=pltpu.SMEM)
F32 = jnp.float32
BF16 = jnp.bfloat16


def passed_along(x, axis, by):
    devices = lax.axis_size(axis)
    return lax.ppermute(x, axis, [(i, (i + by) % devices) for i in range(devices)])


def nt(left, right):
    return lax.dot_general(left, right, (((1,), (1,)), ((), ())), preferred_element_type=F32)


def tn(left, right):
    return lax.dot_general(left, right, (((0,), (0,)), ((), ())), preferred_element_type=F32)


def nn(left, right):
    return lax.dot_general(left, right, (((1,), (0,)), ((), ())), preferred_element_type=F32)


def tile_logits(scal, texts, images):
    return scal[0] * nt(texts, images) + scal[1]


def small(logits):
    return jnp.exp(-jnp.abs(logits))


def sigmoid(logits, e):
    return jnp.where(logits >= 0.0, 1.0, e) / (1.0 + e)


def softplus(v, e):
    return jnp.maximum(v, 0.0) + jnp.log1p(e)


def image_side(scal, images, far_texts):
    logits = tile_logits(scal, far_texts, images)
    e = small(logits)
    coeff = (scal[0] * sigmoid(logits, e)).astype(BF16)
    return jnp.sum(softplus(logits, e), axis=0, keepdims=True), tn(coeff, far_texts)


def text_side(scal, texts, far_images):
    logits = tile_logits(scal, texts, far_images)
    coeff = (scal[0] * sigmoid(logits, small(logits))).astype(BF16)
    return nn(coeff, far_images)


def own_kernel(scal, pos_ref, images_ref, texts_ref, loss_ref, igrad_ref, tgrad_ref):
    images, texts = images_ref[...], texts_ref[...]
    logits = tile_logits(scal, texts, images)
    mask = pos_ref[...] == lax.broadcasted_iota(jnp.int32, logits.shape, 0)
    e = small(logits)
    loss_ref[...] = jnp.sum(
        softplus(jnp.where(mask, -logits, logits), e), axis=0, keepdims=True
    )
    coeff = (scal[0] * (sigmoid(logits, e) - jnp.where(mask, 1.0, 0.0))).astype(BF16)
    igrad_ref[...] = tn(coeff, texts)
    tgrad_ref[...] = nn(coeff, images)


def pick_kernel(role, images_ref, texts_ref, out_ref, sem):
    @pl.when(role[0] != 0)
    def _():
        copy = pltpu.make_async_copy(texts_ref, out_ref, sem)
        copy.start()
        copy.wait()

    @pl.when(role[0] == 0)
    def _():
        copy = pltpu.make_async_copy(images_ref, out_ref, sem)
        copy.start()
        copy.wait()


def link_kernel(
    scal, role, images_ref, texts_ref, far_ref, loss_in, igrad_in, tgrad_in,
    loss_ref, igrad_ref, tgrad_ref,
):
    @pl.when(role[0] == 0)
    def _():
        loss, grad = image_side(scal, images_ref[...], far_ref[...])
        loss_ref[...] = loss_in[...] + loss
        igrad_ref[...] = igrad_in[...] + grad
        tgrad_ref[...] = tgrad_in[...]

    @pl.when(role[0] != 0)
    def _():
        loss_ref[...] = loss_in[...]
        igrad_ref[...] = igrad_in[...]
        tgrad_ref[...] = tgrad_in[...] + text_side(scal, texts_ref[...], far_ref[...])


def dp_text_kernel(scal, images_ref, far_texts_ref, loss_in, igrad_in, loss_ref, igrad_ref):
    loss, grad = image_side(scal, images_ref[...], far_texts_ref[...])
    loss_ref[...] = loss_in[...] + loss
    igrad_ref[...] = igrad_in[...] + grad


def chip_kernel(
    scal, role, images_ref, texts_ref, far_ref, loss_in, igrad_in, tgrad_in,
    loss_ref, igrad_out, tgrad_ref, igrad_ref, sem,
):
    def send():
        return pltpu.make_async_copy(igrad_ref, igrad_out, sem)

    @pl.when(role[0] != 0)
    def _():
        loss, grad = image_side(scal, images_ref[...], far_ref[...])
        loss_ref[...] = loss_in[...] + loss
        igrad_ref[...] = (igrad_in[...] + grad).astype(BF16)
        send().start()
        tgrad_ref[...] = tgrad_in[...]

    @pl.when(role[0] == 0)
    def _():
        loss_ref[...] = loss_in[...]
        igrad_ref[...] = igrad_in[...].astype(BF16)
        send().start()
        tgrad_ref[...] = tgrad_in[...] + text_side(scal, texts_ref[...], far_ref[...])

    send().wait()


def last_kernel(scal, texts_ref, far_images_ref, loss_in, tgrad_in, loss_ref, tgrad_ref):
    loss_ref[...] = loss_in[...] / (3.0 * loss_in.shape[1])
    grad = text_side(scal, texts_ref[...], far_images_ref[...])
    tgrad_ref[...] = (tgrad_in[...] + grad).astype(BF16)


def call(kernel, outs, scalars, *args, in_specs=None, out_specs=None, scratch=(), room=40):
    return pl.pallas_call(
        kernel,
        out_shape=outs,
        in_specs=[SMEM] * len(scalars) + (in_specs or [VMEM] * len(args)),
        out_specs=out_specs or [VMEM] * len(outs),
        scratch_shapes=scratch,
        compiler_params=pltpu.CompilerParams(vmem_limit_bytes=room * 1024 * 1024),
        cost_estimate=pl.CostEstimate(flops=1000, bytes_accessed=1000, transcendentals=0),
    )(*scalars, *args)


def local(images, texts, positive_index, log_scale, bias):
    rows, width = images.shape
    outer = lax.axis_size("outer")
    core = lax.axis_index("outer") % 2
    role = core.astype(jnp.int32).reshape(1)
    scal = jnp.concatenate([jnp.exp(log_scale), bias])
    loss_shape = jax.ShapeDtypeStruct((1, rows), F32)
    wide = jax.ShapeDtypeStruct((rows, width), F32)
    narrow = jax.ShapeDtypeStruct((rows, width), BF16)
    away = pl.BlockSpec(memory_space=pl.ANY)

    def swap(x, shift):
        pairs = [((o + shift) % outer, (o + 1 + shift) % outer) for o in range(0, outer, 2)]
        return lax.ppermute(x, "outer", pairs + [(b, a) for a, b in pairs])

    (over_link,) = call(
        pick_kernel, [narrow], [role], images, texts,
        in_specs=[away, away], scratch=[pltpu.SemaphoreType.DMA(())], room=40,
    )
    over_link, texts, images = lax.optimization_barrier((over_link, texts, images))
    link = swap(over_link, 1)
    cycle_text = passed_along(texts, "dp", 1)
    chip = swap(jnp.where(core == 0, texts, images), 0)
    cycle_images = passed_along(images, "dp", -1)

    sums = call(own_kernel, [loss_shape, wide, wide], [scal], positive_index, images, texts)
    loss, igrad, tgrad = call(
        link_kernel, [loss_shape, wide, wide], [scal, role], images, texts, link, *sums
    )
    loss, igrad = call(
        dp_text_kernel, [loss_shape, wide], [scal], images, cycle_text, loss, igrad
    )
    loss, igrad, tgrad = call(
        chip_kernel, [loss_shape, narrow, wide], [scal, role],
        images, texts, chip, loss, igrad, tgrad,
        out_specs=[VMEM, away, VMEM],
        scratch=[pltpu.VMEM((rows, width), BF16), pltpu.SemaphoreType.DMA(())],
    )
    loss, tgrad = call(
        last_kernel, [loss_shape, narrow], [scal], texts, cycle_images, loss, tgrad
    )
    return loss.reshape(rows), igrad, tgrad


def solution(mesh):
    in_specs = (
        P(("dp", "outer"), None),
        P(("dp", "outer"), None),
        P(("dp", "outer"), None),
        P(),
        P(),
    )
    out_specs = (P(("dp", "outer")), P(("dp", "outer"), None), P(("dp", "outer"), None))
    return jax.shard_map(local, mesh=mesh, in_specs=in_specs, out_specs=out_specs, check_vma=False)
```

```python
import jax
import jax.numpy as jnp
from jax import lax
from jax.experimental import pallas as pl
from jax.experimental.pallas import tpu as pltpu
from jax.sharding import PartitionSpec as P

VMEM = pl.BlockSpec(memory_space=pltpu.VMEM)
SMEM = pl.BlockSpec(memory_space=pltpu.SMEM)
F32 = jnp.float32
BF16 = jnp.bfloat16


def passed_along(x, axis, by):
    devices = lax.axis_size(axis)
    return lax.ppermute(x, axis, [(i, (i + by) % devices) for i in range(devices)])


def nt(left, right):
    return lax.dot_general(left, right, (((1,), (1,)), ((), ())), preferred_element_type=F32)


def tn(left, right):
    return lax.dot_general(left, right, (((0,), (0,)), ((), ())), preferred_element_type=F32)


def nn(left, right):
    return lax.dot_general(left, right, (((1,), (0,)), ((), ())), preferred_element_type=F32)


def tile_logits(scal, texts, images):
    return scal[0] * nt(texts, images) + scal[1]


def small(logits):
    return jnp.exp(-jnp.abs(logits))


def sigmoid(logits, e):
    return jnp.where(logits >= 0.0, 1.0, e) / (1.0 + e)


def softplus(v, e):
    return jnp.maximum(v, 0.0) + jnp.log1p(e)


def image_side(scal, images, far_texts):
    logits = tile_logits(scal, far_texts, images)
    e = small(logits)
    coeff = (scal[0] * sigmoid(logits, e)).astype(BF16)
    return jnp.sum(softplus(logits, e), axis=0, keepdims=True), tn(coeff, far_texts)


def text_side(scal, texts, far_images):
    logits = tile_logits(scal, texts, far_images)
    coeff = (scal[0] * sigmoid(logits, small(logits))).astype(BF16)
    return nn(coeff, far_images)


def own_kernel(scal, pos_ref, images_ref, texts_ref, loss_ref, igrad_ref, tgrad_ref):
    images, texts = images_ref[...], texts_ref[...]
    logits = tile_logits(scal, texts, images)
    mask = pos_ref[...] == lax.broadcasted_iota(jnp.int32, logits.shape, 0)
    e = small(logits)
    loss_ref[...] = jnp.sum(
        softplus(jnp.where(mask, -logits, logits), e), axis=0, keepdims=True
    )
    coeff = (scal[0] * (sigmoid(logits, e) - jnp.where(mask, 1.0, 0.0))).astype(BF16)
    igrad_ref[...] = tn(coeff, texts)
    tgrad_ref[...] = nn(coeff, images)


def pick_kernel(role, images_ref, texts_ref, out_ref, sem):
    @pl.when(role[0] != 0)
    def _():
        copy = pltpu.make_async_copy(texts_ref, out_ref, sem)
        copy.start()
        copy.wait()

    @pl.when(role[0] == 0)
    def _():
        copy = pltpu.make_async_copy(images_ref, out_ref, sem)
        copy.start()
        copy.wait()


def link_kernel(
    scal, role, images_ref, texts_ref, far_ref, loss_in, igrad_in, tgrad_in,
    loss_ref, igrad_ref, tgrad_ref,
):
    @pl.when(role[0] == 0)
    def _():
        loss, grad = image_side(scal, images_ref[...], far_ref[...])
        loss_ref[...] = loss_in[...] + loss
        igrad_ref[...] = igrad_in[...] + grad
        tgrad_ref[...] = tgrad_in[...]

    @pl.when(role[0] != 0)
    def _():
        loss_ref[...] = loss_in[...]
        igrad_ref[...] = igrad_in[...]
        tgrad_ref[...] = tgrad_in[...] + text_side(scal, texts_ref[...], far_ref[...])


def chip_kernel(
    scal, role, images_ref, texts_ref, far_a, far_b, loss_in, igrad_in, tgrad_in,
    loss_ref, igrad_ref, tgrad_ref,
):
    @pl.when(role[0] != 0)
    def _():
        loss_a, grad_a = image_side(scal, images_ref[...], far_a[...])
        loss_b, grad_b = image_side(scal, images_ref[...], far_b[...])
        loss_ref[...] = loss_in[...] + loss_a + loss_b
        igrad_ref[...] = igrad_in[...] + grad_a + grad_b
        tgrad_ref[...] = tgrad_in[...]

    @pl.when(role[0] == 0)
    def _():
        loss_ref[...] = loss_in[...]
        igrad_ref[...] = igrad_in[...]
        grad = text_side(scal, texts_ref[...], far_a[...])
        tgrad_ref[...] = tgrad_in[...] + grad + text_side(scal, texts_ref[...], far_b[...])


def last_kernel(
    scal, images_ref, texts_ref, far_texts_ref, far_images_ref, loss_in, igrad_in, tgrad_in,
    loss_ref, igrad_out, tgrad_out, igrad_ref, tgrad_ref, sems,
):
    loss, grad = image_side(scal, images_ref[...], far_texts_ref[...])
    loss_ref[...] = (loss_in[...] + loss) / (3.0 * loss_in.shape[1])
    igrad_ref[...] = (igrad_in[...] + grad).astype(BF16)
    image_copy = pltpu.make_async_copy(igrad_ref, igrad_out, sems.at[0])
    image_copy.start()
    grad = text_side(scal, texts_ref[...], far_images_ref[...])
    tgrad_ref[...] = (tgrad_in[...] + grad).astype(BF16)
    text_copy = pltpu.make_async_copy(tgrad_ref, tgrad_out, sems.at[1])
    text_copy.start()
    image_copy.wait()
    text_copy.wait()


def call(kernel, outs, scalars, *args, in_specs=None, out_specs=None, scratch=()):
    return pl.pallas_call(
        kernel,
        out_shape=outs,
        in_specs=[SMEM] * len(scalars) + (in_specs or [VMEM] * len(args)),
        out_specs=out_specs or [VMEM] * len(outs),
        scratch_shapes=scratch,
        compiler_params=pltpu.CompilerParams(vmem_limit_bytes=40 * 1024 * 1024),
        cost_estimate=pl.CostEstimate(flops=1000, bytes_accessed=1000, transcendentals=0),
    )(*scalars, *args)


def local(images, texts, positive_index, log_scale, bias):
    rows, width = images.shape
    outer = lax.axis_size("outer")
    core = lax.axis_index("outer") % 2
    role = core.astype(jnp.int32).reshape(1)
    scal = jnp.concatenate([jnp.exp(log_scale), bias])
    loss_shape = jax.ShapeDtypeStruct((1, rows), F32)
    wide = jax.ShapeDtypeStruct((rows, width), F32)
    narrow = jax.ShapeDtypeStruct((rows, width), BF16)
    away = pl.BlockSpec(memory_space=pl.ANY)

    def swap(x, shift):
        pairs = [((o + shift) % outer, (o + 1 + shift) % outer) for o in range(0, outer, 2)]
        return lax.ppermute(x, "outer", pairs + [(b, a) for a, b in pairs])

    (over_link,) = call(
        pick_kernel, [narrow], [role], images, texts,
        in_specs=[away, away], scratch=[pltpu.SemaphoreType.DMA(())],
    )
    over_link, texts, images = lax.optimization_barrier((over_link, texts, images))
    link = swap(over_link, 1)
    cycle_text = passed_along(texts, "dp", 1)
    cut = rows // 2
    over_chip = jnp.where(core == 0, texts, images)
    chip = [swap(x, 0) for x in (over_chip[:cut], over_chip[cut:])]
    cycle_images = passed_along(images, "dp", -1)

    sums = call(own_kernel, [loss_shape, wide, wide], [scal], positive_index, images, texts)
    sums = call(link_kernel, [loss_shape, wide, wide], [scal, role], images, texts, link, *sums)
    sums = call(chip_kernel, [loss_shape, wide, wide], [scal, role], images, texts, *chip, *sums)
    held = pltpu.VMEM((rows, width), BF16)
    loss, igrad, tgrad = call(
        last_kernel, [loss_shape, narrow, narrow], [scal],
        images, texts, cycle_text, cycle_images, *sums,
        out_specs=[VMEM, away, away],
        scratch=[held, held, pltpu.SemaphoreType.DMA((2,))],
    )
    return loss.reshape(rows), igrad, tgrad


def solution(mesh):
    in_specs = (
        P(("dp", "outer"), None),
        P(("dp", "outer"), None),
        P(("dp", "outer"), None),
        P(),
        P(),
    )
    out_specs = (P(("dp", "outer")), P(("dp", "outer"), None), P(("dp", "outer"), None))
    return jax.shard_map(local, mesh=mesh, in_specs=in_specs, out_specs=out_specs, check_vma=False)
```

```python
import jax
import jax.numpy as jnp
from jax import lax
from jax.experimental import pallas as pl
from jax.experimental.pallas import tpu as pltpu
from jax.sharding import PartitionSpec as P

VMEM = pl.BlockSpec(memory_space=pltpu.VMEM)
SMEM = pl.BlockSpec(memory_space=pltpu.SMEM)
F32 = jnp.float32
BF16 = jnp.bfloat16


def passed_along(x, axis, by):
    devices = lax.axis_size(axis)
    return lax.ppermute(x, axis, [(i, (i + by) % devices) for i in range(devices)])


def nt(left, right):
    return lax.dot_general(left, right, (((1,), (1,)), ((), ())), preferred_element_type=F32)


def tn(left, right):
    return lax.dot_general(left, right, (((0,), (0,)), ((), ())), preferred_element_type=F32)


def nn(left, right):
    return lax.dot_general(left, right, (((1,), (0,)), ((), ())), preferred_element_type=F32)


def tile_logits(scal, texts, images):
    return scal[0] * nt(texts, images) + scal[1]


def small(logits):
    return jnp.exp(-jnp.abs(logits))


def sigmoid(logits, e):
    return jnp.where(logits >= 0.0, 1.0, e) / (1.0 + e)


def softplus(v, e):
    return jnp.maximum(v, 0.0) + jnp.log1p(e)


def image_side(scal, images, far_texts):
    logits = tile_logits(scal, far_texts, images)
    e = small(logits)
    coeff = (scal[0] * sigmoid(logits, e)).astype(BF16)
    return jnp.sum(softplus(logits, e), axis=0, keepdims=True), tn(coeff, far_texts)


def text_side(scal, texts, far_images):
    logits = tile_logits(scal, texts, far_images)
    coeff = (scal[0] * sigmoid(logits, small(logits))).astype(BF16)
    return nn(coeff, far_images)


def own_kernel(
    scal, pos_ref, images_ref, texts_ref, loss_ref, igrad_ref, tgrad_ref, images_kept, texts_kept
):
    images, texts = images_ref[...], texts_ref[...]
    images_kept[...] = images
    texts_kept[...] = texts
    logits = tile_logits(scal, texts, images)
    mask = pos_ref[...] == lax.broadcasted_iota(jnp.int32, logits.shape, 0)
    e = small(logits)
    loss_ref[...] = jnp.sum(
        softplus(jnp.where(mask, -logits, logits), e), axis=0, keepdims=True
    )
    coeff = (scal[0] * (sigmoid(logits, e) - jnp.where(mask, 1.0, 0.0))).astype(BF16)
    igrad_ref[...] = tn(coeff, texts)
    tgrad_ref[...] = nn(coeff, images)


def pick_kernel(role, images_ref, texts_ref, out_ref, sem):
    @pl.when(role[0] != 0)
    def _():
        copy = pltpu.make_async_copy(texts_ref, out_ref, sem)
        copy.start()
        copy.wait()

    @pl.when(role[0] == 0)
    def _():
        copy = pltpu.make_async_copy(images_ref, out_ref, sem)
        copy.start()
        copy.wait()


def link_kernel(
    scal, role, images_ref, texts_ref, far_ref, loss_in, igrad_in, tgrad_in,
    loss_ref, igrad_ref, tgrad_ref,
):
    @pl.when(role[0] == 0)
    def _():
        loss, grad = image_side(scal, images_ref[...], far_ref[...])
        loss_ref[...] = loss_in[...] + loss
        igrad_ref[...] = igrad_in[...] + grad
        tgrad_ref[...] = tgrad_in[...]

    @pl.when(role[0] != 0)
    def _():
        loss_ref[...] = loss_in[...]
        igrad_ref[...] = igrad_in[...]
        tgrad_ref[...] = tgrad_in[...] + text_side(scal, texts_ref[...], far_ref[...])


def chip_kernel(
    scal, role, images_ref, texts_ref, far_a, far_b, loss_in, igrad_in, tgrad_in,
    loss_ref, igrad_ref, tgrad_ref,
):
    @pl.when(role[0] != 0)
    def _():
        loss_a, grad_a = image_side(scal, images_ref[...], far_a[...])
        loss_b, grad_b = image_side(scal, images_ref[...], far_b[...])
        loss_ref[...] = loss_in[...] + loss_a + loss_b
        igrad_ref[...] = igrad_in[...] + grad_a + grad_b
        tgrad_ref[...] = tgrad_in[...]

    @pl.when(role[0] == 0)
    def _():
        loss_ref[...] = loss_in[...]
        igrad_ref[...] = igrad_in[...]
        grad = text_side(scal, texts_ref[...], far_a[...])
        tgrad_ref[...] = tgrad_in[...] + grad + text_side(scal, texts_ref[...], far_b[...])


def last_kernel(
    scal, images_ref, texts_ref, far_texts_ref, far_images_ref, loss_in, igrad_in, tgrad_in,
    loss_ref, igrad_out, tgrad_out, igrad_ref, tgrad_ref, sems,
):
    loss, grad = image_side(scal, images_ref[...], far_texts_ref[...])
    loss_ref[...] = (loss_in[...] + loss) / (3.0 * loss_in.shape[1])
    igrad_ref[...] = (igrad_in[...] + grad).astype(BF16)
    image_copy = pltpu.make_async_copy(igrad_ref, igrad_out, sems.at[0])
    image_copy.start()
    grad = text_side(scal, texts_ref[...], far_images_ref[...])
    tgrad_ref[...] = (tgrad_in[...] + grad).astype(BF16)
    text_copy = pltpu.make_async_copy(tgrad_ref, tgrad_out, sems.at[1])
    text_copy.start()
    image_copy.wait()
    text_copy.wait()


def call(kernel, outs, scalars, *args, in_specs=None, out_specs=None, scratch=()):
    return pl.pallas_call(
        kernel,
        out_shape=outs,
        in_specs=[SMEM] * len(scalars) + (in_specs or [VMEM] * len(args)),
        out_specs=out_specs or [VMEM] * len(outs),
        scratch_shapes=scratch,
        compiler_params=pltpu.CompilerParams(vmem_limit_bytes=40 * 1024 * 1024),
        cost_estimate=pl.CostEstimate(flops=1000, bytes_accessed=1000, transcendentals=0),
    )(*scalars, *args)


def local(images, texts, positive_index, log_scale, bias):
    rows, width = images.shape
    outer = lax.axis_size("outer")
    core = lax.axis_index("outer") % 2
    role = core.astype(jnp.int32).reshape(1)
    scal = jnp.concatenate([jnp.exp(log_scale), bias])
    loss_shape = jax.ShapeDtypeStruct((1, rows), F32)
    wide = jax.ShapeDtypeStruct((rows, width), F32)
    narrow = jax.ShapeDtypeStruct((rows, width), BF16)
    away = pl.BlockSpec(memory_space=pl.ANY)

    def swap(x, shift):
        pairs = [((o + shift) % outer, (o + 1 + shift) % outer) for o in range(0, outer, 2)]
        return lax.ppermute(x, "outer", pairs + [(b, a) for a, b in pairs])

    (over_link,) = call(
        pick_kernel, [narrow], [role], images, texts,
        in_specs=[away, away], scratch=[pltpu.SemaphoreType.DMA(())],
    )
    over_link, texts, images = lax.optimization_barrier((over_link, texts, images))
    link = swap(over_link, 1)
    cycle_text = passed_along(texts, "dp", 1)
    cut = rows // 2
    over_chip = jnp.where(core == 0, texts, images)
    chip = [swap(x, 0) for x in (over_chip[:cut], over_chip[cut:])]
    cycle_images = passed_along(images, "dp", -1)

    *sums, images, texts = call(
        own_kernel, [loss_shape, wide, wide, narrow, narrow], [scal],
        positive_index, images, texts,
    )
    sums = call(link_kernel, [loss_shape, wide, wide], [scal, role], images, texts, link, *sums)
    sums = call(chip_kernel, [loss_shape, wide, wide], [scal, role], images, texts, *chip, *sums)
    held = pltpu.VMEM((rows, width), BF16)
    loss, igrad, tgrad = call(
        last_kernel, [loss_shape, narrow, narrow], [scal],
        images, texts, cycle_text, cycle_images, *sums,
        out_specs=[VMEM, away, away],
        scratch=[held, held, pltpu.SemaphoreType.DMA((2,))],
    )
    return loss.reshape(rows), igrad, tgrad


def solution(mesh):
    in_specs = (
        P(("dp", "outer"), None),
        P(("dp", "outer"), None),
        P(("dp", "outer"), None),
        P(),
        P(),
    )
    out_specs = (P(("dp", "outer")), P(("dp", "outer"), None), P(("dp", "outer"), None))
    return jax.shard_map(local, mesh=mesh, in_specs=in_specs, out_specs=out_specs, check_vma=False)
```
